32 devices in a mesh: group: 2 (over y), inst: 4 (over x, core), brick: 4 (over z).
Axes of the slice: x: 2, y: 2, z: 4, core: 2. Of those that a mesh axis runs over, the one named last changes fastest.
Arguments:
- state: float32 [32, 5, 32, 4096], P(('group', 'inst'), None, 'brick'), parts along dimension 0, may hold values from -1.5 to 4, as said below
- time_step: float32 [64, 4096], P(('group', 'brick')), parts along dimension 0, may hold values from 0.05 to 0.5
- blocks: bfloat16 [8, 320, 320], replicated, may hold values from -0.3125 to 0.3125
- cut_counts: int32 [8], P('group'), parts along dimension 0, may hold values from 1 to 256, 384 in all
- tile_index: int32 [8, 256], P(('group', 'brick')), parts along dimension 0, may hold values from 0 to 511, as said below
- tile_type: int32 [8, 256], P(('group', 'brick')), parts along dimension 0, may hold values from 0 to 7
Outputs:
- residual: float32 [32, 5, 32, 4096], P(('group', 'inst'), None, 'brick'), parts along dimension 0
- new_state: float32 [32, 5, 32, 4096], P(('group', 'inst'), None, 'brick'), parts along dimension 0
The draws below stay inside these ranges and needn't reach their ends.
There are 2 independent parts, one for each index of `group`. The reference program is written for one: setup_inputs(seed, part) draws one part's arguments, and reference() takes and returns one part's arrays. A program takes and returns all parts, laid end to end along the dimension named above; an argument that names none is the same for every part. Nothing has to cross between parts.
Inputs may be any that keep to these rules, and one draw needn't show every extreme that they name: `state`: component 0 (density) lies in 0.5 to 2, components 1 to 3 in -1.5 to 1.5, component 4 in 1.5 to 4. `tile_index`: row b lists 256 different tiles of brick b. `cut_counts`: the entries sum to 384.
All inputs are finite; a program needn't handle non-finite values.
Results may differ from the reference program's by a relative error of at most 0.0013.
Values may be sent and summed in bfloat16 or wider, within the bound.
A program may use at most 64 MiB of HBM per device.

```python
import math
import jax
import jax.numpy as jnp
import numpy as np
from jax import lax

NINST = 16
NVAR = 5
TILE = 64
KTYPES = 8
CS = 4096
NX = 32
TSIZE = 320
TILES_DEV = 512
TCAP = 256
CUT_MEAN = 96
N_BRICK = 4


def draw_state(key, part):
    shape = (NINST, NX, CS)
    key_one, key_two, key_three = jax.random.split(key, 3)
    density = jax.random.uniform(key_one, shape, jnp.float32, 0.5, 2.0)
    energy = jax.random.uniform(key_three, shape, jnp.float32, 1.5, 4.0)
    momentum = jnp.clip(0.5 * jax.random.normal(key_two, (3,) + shape, jnp.float32), -1.5, 1.5)
    return jnp.concatenate([density[:, None], jnp.transpose(momentum, (1, 0, 2, 3)), energy[:, None]], axis=1)


def draw_tile_index(key, part):
    keys = jax.random.split(key, N_BRICK + 1)
    where_to = jax.random.randint(keys[N_BRICK], (), 0, TCAP)

    def one_row(row_key, row):
        order = jax.random.permutation(row_key, TILES_DEV).astype(jnp.int32)
        found = jnp.argmax(order == TILES_DEV - 1).astype(jnp.int32)
        moved = jnp.roll(order, where_to - found)
        chosen = jnp.where(row == 0, moved, order)
        return chosen[:TCAP]
    return jax.vmap(one_row)(keys[:N_BRICK], jnp.arange(N_BRICK, dtype=jnp.int32))


def plant(entries, key, low, high):
    place = [jax.random.randint(jax.random.fold_in(key, axis), (), 0, length) for axis, length in enumerate(entries.shape)]
    longest = entries.shape.index(max(entries.shape))
    neighbour = place[:longest] + [(place[longest] + 1) % entries.shape[longest]] + place[longest + 1:]
    return entries.at[tuple(place)].set(low).at[tuple(neighbour)].set(high)


def block_levels(key, shape, pieces, least, high):
    def one(axis_at, blocks):
        heights = jax.random.uniform(jax.random.fold_in(jax.random.fold_in(key, 6), axis_at), (blocks,), jnp.float32, least / len(pieces), high / len(pieces))
        return jnp.repeat(jnp.exp(heights), shape[axis_at] // blocks).reshape((-1,) + (1,) * (len(shape) - axis_at - 1))

    loudness = one(*pieces[0])
    for cut in pieces[1:]:
        loudness = loudness * one(*cut)
    return loudness


def length_profile(number_of, total, bound, slope):
    loads = [(1 << 20) // math.isqrt(grade ** slope) + 1 for grade in range(2, number_of + 1)]
    spare, counts = total - bound - (number_of - 1), [1] * (number_of - 1)
    while spare > 0:
        candidates = [i for i in range(number_of - 1) if counts[i] < bound]
        whole, left = sum([loads[i] for i in candidates]), spare
        for i in candidates:
            extra = min(bound - counts[i], max(1, left * loads[i] // whole), spare)
            counts[i] = counts[i] + extra
            spare = spare - extra
    return np.array([bound] + counts)


def uneven(rng, count, total, bound, lean):
    if count == 2:
        one = jax.random.randint(rng, (), max(1, total - bound), min(bound, total - 1) + 1)
        return jnp.stack([one, total - one])
    tallies = jnp.asarray(length_profile(count, total, bound, lean), jnp.int32)
    couples = (count - 1) // 2
    giver, receiver = tallies[1:1 + 2 * couples:2], tallies[2:2 + 2 * couples:2]
    margin = jnp.minimum(giver - 1, bound - receiver)
    moved = jax.random.randint(jax.random.fold_in(rng, 1), (couples,), 0, 1 << 20) % (margin + 1)
    tallies = tallies.at[1:1 + 2 * couples:2].set(giver - moved).at[2:2 + 2 * couples:2].set(receiver + moved)
    return tallies[jax.random.permutation(jax.random.fold_in(rng, 2), count)]


def centred(rng, extent, deviation, bound, kind=jnp.bfloat16):
    array = deviation * jax.random.normal(rng, extent, jnp.float32)
    return jnp.clip(array, min=-bound, max=bound).astype(kind)


def setup_inputs(seed: int = 0, part: int = 0) -> dict:
    streams_of = jax.random.split(jax.random.key(seed), 7)
    own_keys = jax.random.split(jax.random.fold_in(streams_of[6], part), 7)
    state = draw_state(jax.random.fold_in(jax.random.fold_in(streams_of[6], part), 71), part)
    time_step = jnp.clip(jnp.exp(math.log(0.5) - 2.3025851 * jax.random.uniform(own_keys[1], (NX, CS), jnp.float32) ** block_levels(own_keys[1], (NX, CS), ((0, 4),), -0.2, 0.2)), 0.05, 0.5)
    blocks = centred(streams_of[2], (KTYPES, TSIZE, TSIZE), TSIZE ** -0.5, 0.3125)
    cut_counts = uneven(own_keys[3], N_BRICK, N_BRICK * CUT_MEAN, TCAP, 2).astype(jnp.int32)
    tile_index = draw_tile_index(jax.random.fold_in(jax.random.fold_in(streams_of[6], part), 71), part)
    tile_type = plant(jax.random.randint(own_keys[5], (N_BRICK, TCAP), 0, KTYPES), jax.random.fold_in(own_keys[5], 1), 0, KTYPES - 1).astype(jnp.int32)
    return dict(state=state, time_step=time_step, blocks=blocks, cut_counts=cut_counts, tile_index=tile_index, tile_type=tile_type)


GAMMA_MINUS = 0.4
EPS_FOURTH = 0.03125


def spectral_entry(diff, count):
    shifted = jnp.mod(diff, count)
    sign = 1.0 - 2.0 * jnp.mod(diff, 2).astype(jnp.float32)
    safe = jnp.where(shifted == 0, 1, shifted).astype(jnp.float32)
    value = sign / jnp.tan(jnp.pi * safe / count)
    return jnp.where(shifted == 0, 0.0, value).astype(jnp.float32)


def euler_flux(state):
    density = state[:, 0]
    mom_one = state[:, 1]
    mom_two = state[:, 2]
    mom_three = state[:, 3]
    energy = state[:, 4]
    speed = mom_one / density
    press = GAMMA_MINUS * (energy - 0.5 * (mom_one * mom_one + mom_two * mom_two + mom_three * mom_three) / density)
    return jnp.stack([mom_one, mom_one * speed + press, mom_two * speed, mom_three * speed, (energy + press) * speed], axis=1)


def reference(state, time_step, blocks, cut_counts, tile_index, tile_type):
    flux = euler_flux(state)
    wide = jnp.pad(jnp.concatenate([flux, state], axis=1), ((0, 0), (0, 0), (2, 2), (0, 0)))
    fpad = wide[:, :NVAR]
    qpad = wide[:, NVAR:]
    transport = 0.5 * (fpad[:, :, 3:-1] - fpad[:, :, 1:-3])
    smoothing = EPS_FOURTH * (qpad[:, :, 4:] - 4.0 * qpad[:, :, 3:-1] + 6.0 * qpad[:, :, 2:-2] - 4.0 * qpad[:, :, 1:-3] + qpad[:, :, :-4])
    every = jnp.arange(NINST, dtype=jnp.int32)
    dmat = spectral_entry(every[:, None] - every[None, :], NINST)
    timewise = jnp.einsum('jk,kcxs->jcxs', dmat, state, precision=lax.Precision.HIGHEST)
    tiles = state.reshape(NINST, NVAR, N_BRICK, TILES_DEV, TILE).transpose(2, 3, 0, 1, 4).reshape(N_BRICK, TILES_DEV, NINST, TSIZE)
    slots = jnp.arange(TCAP, dtype=jnp.int32)

    def one_brick(inputs):
        brick_tiles, index_row, type_row, count = inputs
        chosen = brick_tiles[index_row].astype(jnp.bfloat16)
        kinds = blocks[type_row]
        prod = jnp.einsum('tab,tib->tia', kinds.astype(jnp.float32), chosen.astype(jnp.float32), precision=lax.Precision.HIGHEST)
        prod = jnp.where((slots < count)[:, None, None], prod, 0.0)
        return jnp.zeros((TILES_DEV, NINST, TSIZE), jnp.float32).at[index_row].add(prod)

    cut_tiles = lax.map(one_brick, (tiles, tile_index, tile_type, cut_counts))
    cut = cut_tiles.reshape(N_BRICK, TILES_DEV, NINST, NVAR, TILE).transpose(2, 3, 0, 1, 4).reshape(NINST, NVAR, NX, CS)
    residual = transport + smoothing + cut + timewise
    new_state = state - time_step[None, None] * residual
    return residual, new_state
```

```python
import functools
import math

import jax
import jax.numpy as jnp
from jax import lax
from jax.experimental import pallas as pl
from jax.experimental.pallas import tpu as pltpu
from jax.sharding import PartitionSpec as P

MESH = pl.DeviceIdType.MESH
GAMMA_MINUS = 0.4
EPS_FOURTH = 0.03125
CENTRE = (1.25, 0.0, 0.0, 0.0, 2.75)
LANES = 128


def spectral(m, count):
    m = m % count
    if m == 0 or 2 * m == count:
        return 0.0
    return (-1.0) ** m / math.tan(math.pi * m / count)


def flux_of(q):
    den, one, two, three, energy = q
    inv = 1.0 / den
    speed = one * inv
    press = GAMMA_MINUS * (energy - 0.5 * (one * one + two * two + three * three) * inv)
    return (one, one * speed + press, two * speed, three * speed, (energy + press) * speed)


def kernel(
    sizes, state, step, blocks, counts, index, kinds, res_out, new_out,
    x, sib, send, cross, fwd, halo_out, halo_in, wide, xs, lhs, km, acc, fresh,
    in_sem, sib_send, sib_recv, cross_send, cross_recv, fwd_send, fwd_recv, halo_send, halo_recv, out_sem,
):
    inst, nvar, rows, cells, tile, total, chunks, n_brick = sizes
    width = cells // chunks
    ntypes = blocks.shape[0]
    group = lax.axis_index("group")
    me = lax.axis_index("inst")
    brick = lax.axis_index("brick")
    core = lax.rem(me, 2)
    chip = me // 2
    sibling = (group, chip * 2 + (1 - core), brick)
    partner = (group, (1 - chip) * 2 + core, brick)
    below = (group, me, brick - 1)
    above = (group, me, brick + 1)
    has_below = brick > 0
    has_above = brick < n_brick - 1

    def lanes(c):
        return pl.ds(pl.multiple_of(c * width, LANES), width)

    def fetch(c):
        return pltpu.make_async_copy(state.at[:, lanes(c)], x.at[:, lanes(c)], in_sem.at[c])

    def to_sibling(c):
        return pltpu.make_async_remote_copy(
            x.at[:, lanes(c)], sib.at[:, lanes(c)], sib_send.at[c], sib_recv.at[c], sibling, device_id_type=MESH)

    def to_partner(c):
        return pltpu.make_async_remote_copy(
            send.at[c], cross.at[c], cross_send.at[c], cross_recv.at[c], partner, device_id_type=MESH)

    def forward(c):
        return pltpu.make_async_remote_copy(
            cross.at[c], fwd.at[c], fwd_send.at[c], fwd_recv.at[c], sibling, device_id_type=MESH)

    def halo(side):
        return pltpu.make_async_remote_copy(
            halo_out.at[side], halo_in.at[side], halo_send.at[side], halo_recv.at[side],
            below if side == 0 else above, device_id_type=MESH)

    @pl.loop(0, chunks)
    def _(c):
        fetch(c).start()

    barrier = pltpu.get_barrier_semaphore()
    pl.semaphore_signal(barrier, inc=1, device_id=sibling, device_id_type=MESH)
    pl.semaphore_signal(barrier, inc=1, device_id=partner, device_id_type=MESH)

    @pl.when(has_below)
    def _():
        pl.semaphore_signal(barrier, inc=1, device_id=below, device_id_type=MESH)

    @pl.when(has_above)
    def _():
        pl.semaphore_signal(barrier, inc=1, device_id=above, device_id_type=MESH)

    ends = n_brick - 1
    pl.semaphore_wait(barrier, 2 + (brick + ends) // n_brick + (ends - brick + ends) // n_brick)

    @pl.loop(0, chunks)
    def _(c):
        fetch(c).wait()
        for v in range(nvar):
            block = jnp.concatenate(
                [x[(i * nvar + v) * rows:(i * nvar + v + 1) * rows, lanes(c)] for i in range(inst)], axis=0)
            send[c, v * inst * rows:(v + 1) * inst * rows, :] = (block - CENTRE[v]).astype(jnp.bfloat16)
        to_partner(c).start()
        to_sibling(c).start()

    for v in range(nvar):
        for i in range(inst):
            at = (i * nvar + v) * rows
            halo_out[0, v, 2 * i:2 * i + 2, :] = x[at:at + 2, :]
            halo_out[1, v, 2 * i:2 * i + 2, :] = x[at + rows - 2:at + rows, :]

    @pl.when(has_below)
    def _():
        halo(0).start()

    @pl.when(has_above)
    def _():
        halo(1).start()

    per_row = cells // tile
    count = counts[brick]
    slots = index.shape[1]
    where_at = index[...]
    used = lax.broadcasted_iota(jnp.int32, (1, slots), 1) < count
    label = jnp.where(used, kinds[...] + 1, 0).astype(jnp.float32)
    tile_row = where_at // per_row
    tile_col = where_at - tile_row * per_row
    by_row = jnp.where(
        lax.broadcasted_iota(jnp.int32, (rows, slots), 0) == tile_row, label, 0.0).astype(jnp.bfloat16)
    by_col = jnp.where(
        lax.broadcasted_iota(jnp.int32, (per_row, slots), 0) == tile_col, 1.0, 0.0).astype(jnp.bfloat16)
    kind_map = lax.dot_general(
        by_row, by_col, (((1,), (1,)), ((), ())), preferred_element_type=jnp.float32).astype(jnp.bfloat16)
    spread = jnp.where(
        lax.broadcasted_iota(jnp.int32, (per_row, cells), 1) // tile
        == lax.broadcasted_iota(jnp.int32, (per_row, cells), 0), 1.0, 0.0).astype(jnp.bfloat16)
    kind_cells = jnp.dot(kind_map, spread, preferred_element_type=jnp.float32)

    groups = cells // LANES
    for g in range(groups):
        mask = kind_cells[:, g * LANES:(g + 1) * LANES]
        km[g * inst * rows:(g + 1) * inst * rows, :] = jnp.concatenate([mask] * inst, axis=0)
        for v in range(nvar):
            xs[g * inst * rows:(g + 1) * inst * rows, v * LANES:(v + 1) * LANES] = jnp.concatenate(
                [x[(i * nvar + v) * rows:(i * nvar + v + 1) * rows, g * LANES:(g + 1) * LANES]
                 for i in range(inst)], axis=0).astype(jnp.bfloat16)

    first = lax.broadcasted_iota(jnp.int32, (tile, LANES), 1) < tile

    @pl.loop(0, ntypes)
    def _(k):
        for out in range(nvar):
            for v in range(nvar):
                piece = blocks[k, out * tile:(out + 1) * tile, v * tile:(v + 1) * tile].astype(jnp.float32)
                both = jnp.concatenate([piece, piece], axis=1)
                at = out * LANES
                wide[k, at:at + tile, v * LANES:(v + 1) * LANES] = jnp.where(first, both, 0.0).astype(jnp.bfloat16)
                wide[k, at + tile:at + LANES, v * LANES:(v + 1) * LANES] = jnp.where(
                    first, 0.0, both).astype(jnp.bfloat16)

    parts = lhs.shape[0]
    depth = nvar * LANES

    @pl.loop(0, groups * inst * rows // parts)
    def _(m):
        at = pl.ds(pl.multiple_of(m * parts, parts), parts)
        kind_here = km[at, :]
        part = jnp.zeros((parts, depth), jnp.float32)
        for k in range(ntypes):
            keep = jnp.where(kind_here == k + 1.0, 1.0, 0.0).astype(jnp.bfloat16)
            for v in range(nvar):
                lhs[:, v * LANES:(v + 1) * LANES] = xs[at, v * LANES:(v + 1) * LANES] * keep
            part = part + lax.dot_general(
                lhs[...], wide[k], (((1,), (1,)), ((), ())), preferred_element_type=jnp.float32)
        per = parts // (inst * rows)
        for g in range(per):
            to = pl.ds(pl.multiple_of((m * per + g) * LANES, LANES), LANES)
            for i in range(inst):
                for v in range(nvar):
                    acc[(i * nvar + v) * rows:(i * nvar + v + 1) * rows, to] = part[
                        (g * inst + i) * rows:(g * inst + i + 1) * rows, v * LANES:(v + 1) * LANES]

    @pl.when(has_below)
    def _():
        halo(0).wait_send()
        halo(1).wait_recv()

    @pl.when(has_above)
    def _():
        halo(1).wait_send()
        halo(0).wait_recv()

    @pl.when(jnp.logical_not(has_below))
    def _():
        halo_in[1] = jnp.zeros(halo_in.shape[1:], jnp.float32)

    @pl.when(jnp.logical_not(has_above))
    def _():
        halo_in[0] = jnp.zeros(halo_in.shape[1:], jnp.float32)

    near = LANES

    @pl.loop(0, cells // near)
    def _(b):
        at = pl.ds(pl.multiple_of(b * near, LANES), near)
        for i in range(inst):
            full = []
            for v in range(nvar):
                full.append(jnp.concatenate([
                    halo_in[1, v, 2 * i:2 * i + 2, at],
                    x[(i * nvar + v) * rows:(i * nvar + v + 1) * rows, at],
                    halo_in[0, v, 2 * i:2 * i + 2, at],
                ], axis=0))
            safe = [jnp.where(full[0] == 0.0, 1.0, full[0])] + full[1:]
            flux = flux_of(safe)
            for v in range(nvar):
                q, f = full[v], flux[v]
                put = slice((i * nvar + v) * rows, (i * nvar + v + 1) * rows)
                acc[put, at] = acc[put, at] + 0.5 * (f[3:rows + 3] - f[1:rows + 1]) + EPS_FOURTH * (
                    q[4:] - 4.0 * q[3:-1] + 6.0 * q[2:-2] - 4.0 * q[1:-3] + q[:-4])

    def choose(a, b):
        return a if a == b else jnp.where(core == 0, a, b)

    span = range(1 - inst, inst)
    half = total // 2
    d_own = {m: spectral(m, total) for m in span}
    d_sib = {m: choose(spectral(m - inst, total), spectral(m + inst, total)) for m in span}
    d_cross = {m: spectral(m - half, total) for m in span}
    d_fwd = {m: choose(spectral(m - inst - half, total), spectral(m + inst - half, total)) for m in span}

    def finish(c):
        at = lanes(c)
        for v in range(nvar):
            cut = slice(v * inst * rows, (v + 1) * inst * rows)
            one = cross[c, cut, :].astype(jnp.float32)
            two = fwd[c, cut, :].astype(jnp.float32)
            for j in range(inst):
                put = slice((j * nvar + v) * rows, (j * nvar + v + 1) * rows)
                value = acc[put, at]
                for k in range(inst):
                    take = slice((k * nvar + v) * rows, (k * nvar + v + 1) * rows)
                    local = slice(k * rows, (k + 1) * rows)
                    m = j - k
                    if m:
                        value = value + d_own[m] * (x[take, at] - CENTRE[v])
                        value = value + d_cross[m] * one[local]
                    value = value + d_sib[m] * (sib[take, at] - CENTRE[v])
                    value = value + d_fwd[m] * two[local]
                acc[put, at] = value
                fresh[put, at] = x[put, at] - step[:, at] * value
        pltpu.make_async_copy(acc.at[:, at], res_out.at[:, at], out_sem.at[0, c]).start()
        pltpu.make_async_copy(fresh.at[:, at], new_out.at[:, at], out_sem.at[1, c]).start()

    @pl.loop(0, chunks)
    def _(c):
        to_sibling(c).wait()
        to_partner(c).wait()
        forward(c).start()

        @pl.when(c > 0)
        def _():
            forward(c - 1).wait()
            finish(c - 1)

    forward(chunks - 1).wait()
    finish(chunks - 1)

    @pl.loop(0, chunks)
    def _(c):
        at = lanes(c)
        pltpu.make_async_copy(acc.at[:, at], res_out.at[:, at], out_sem.at[0, c]).wait()
        pltpu.make_async_copy(fresh.at[:, at], new_out.at[:, at], out_sem.at[1, c]).wait()


def fused(mesh, state, time_step, blocks, cut_counts, tile_index, tile_type):
    inst, nvar, rows, cells = state.shape
    tile = blocks.shape[1] // nvar
    total = inst * mesh.shape["inst"]
    n_brick = mesh.shape["brick"]
    chunks = 8
    all_rows = inst * nvar * rows
    width = cells // chunks
    depth = nvar * LANES
    product_rows = cells // LANES * inst * rows
    sizes = (inst, nvar, rows, cells, tile, total, chunks, n_brick)
    vmem = pl.BlockSpec(memory_space=pltpu.VMEM)
    hbm = pl.BlockSpec(memory_space=pl.ANY)
    dma = pltpu.SemaphoreType.DMA
    flat = state.reshape(all_rows, cells)
    res, new = pl.pallas_call(
        functools.partial(kernel, sizes),
        out_shape=[jax.ShapeDtypeStruct(flat.shape, jnp.float32)] * 2,
        in_specs=[hbm, vmem, vmem, pl.BlockSpec(memory_space=pltpu.SMEM), vmem, vmem],
        out_specs=[hbm, hbm],
        scratch_shapes=[
            pltpu.VMEM((all_rows, cells), jnp.float32),
            pltpu.VMEM((all_rows, cells), jnp.float32),
            pltpu.VMEM((chunks, all_rows, width), jnp.bfloat16),
            pltpu.VMEM((chunks, all_rows, width), jnp.bfloat16),
            pltpu.VMEM((chunks, all_rows, width), jnp.bfloat16),
            pltpu.VMEM((2, nvar, 2 * inst, cells), jnp.float32),
            pltpu.VMEM((2, nvar, 2 * inst, cells), jnp.float32),
            pltpu.VMEM((blocks.shape[0], depth, depth), jnp.bfloat16),
            pltpu.VMEM((product_rows, depth), jnp.bfloat16),
            pltpu.VMEM((min(256, product_rows), depth), jnp.bfloat16),
            pltpu.VMEM((product_rows, LANES), jnp.float32),
            pltpu.VMEM((all_rows, cells), jnp.float32),
            pltpu.VMEM((all_rows, cells), jnp.float32),
            dma((chunks,)), dma((chunks,)), dma((chunks,)), dma((chunks,)), dma((chunks,)),
            dma((chunks,)), dma((chunks,)), dma((2,)), dma((2,)), dma((2, chunks)),
        ],
        compiler_params=pltpu.CompilerParams(
            collective_id=0, has_side_effects=True, vmem_limit_bytes=48 * 1024 * 1024),
        cost_estimate=pl.CostEstimate(
            flops=2 * product_rows * depth * depth * blocks.shape[0], bytes_accessed=12 * all_rows * cells,
            transcendentals=0),
    )(flat, time_step, blocks, cut_counts, tile_index, tile_type)
    return res.reshape(state.shape), new.reshape(state.shape)


def plain(mesh, state, time_step, blocks, cut_counts, tile_index, tile_type):
    inst, nvar, rows, cells = state.shape
    tile = blocks.shape[1] // nvar
    size = mesh.shape["inst"]
    total = inst * size
    ends = mesh.shape["brick"] - 1
    tail = lax.ppermute(state[:, :, rows - 2:], "brick", [(i, i + 1) for i in range(ends)])
    head = lax.ppermute(state[:, :, :2], "brick", [(i + 1, i) for i in range(ends)])
    q = jnp.concatenate([tail, state, head], axis=2)
    density = jnp.where(q[:, 0] == 0.0, 1.0, q[:, 0])
    f = jnp.stack(flux_of((density, q[:, 1], q[:, 2], q[:, 3], q[:, 4])), axis=1)
    local = 0.5 * (f[:, :, 3:-1] - f[:, :, 1:-3]) + EPS_FOURTH * (
        q[:, :, 4:] - 4.0 * q[:, :, 3:-1] + 6.0 * q[:, :, 2:-2] - 4.0 * q[:, :, 1:-3] + q[:, :, :-4])
    table = jnp.asarray([spectral(m, total) for m in range(total)], jnp.float32)
    mine = lax.axis_index("inst") * inst + jnp.arange(inst)
    timewise = jnp.zeros(state.shape, jnp.float32)
    moving = state
    for hop in range(size):
        source = lax.rem(lax.axis_index("inst") + size - hop, size) * inst + jnp.arange(inst)
        coef = table[jnp.mod(mine[:, None] - source[None, :], total)]
        timewise = timewise + jnp.einsum("jk,kcxs->jcxs", coef, moving, precision=lax.Precision.HIGHEST)
        if hop < size - 1:
            moving = lax.ppermute(moving, "inst", [(i, (i + 1) % size) for i in range(size)])
    tiles = rows * cells // tile
    slots = jnp.arange(tile_index.shape[1])
    used = slots < cut_counts[lax.axis_index("brick")]
    label = jnp.where(used, tile_type[0], blocks.shape[0])
    hot = (tile_index[0][None, :] == jnp.arange(tiles)[:, None]) & used[None, :]
    kind = jnp.where(jnp.any(hot, axis=1), jnp.sum(jnp.where(hot, label[None, :], 0), axis=1), blocks.shape[0])
    by_tile = state.reshape(inst, nvar, tiles, tile).transpose(2, 0, 1, 3).reshape(tiles, inst, nvar * tile)
    by_tile = by_tile.astype(jnp.bfloat16)
    cut = jnp.zeros(by_tile.shape, jnp.float32)
    for k in range(blocks.shape[0]):
        masked = jnp.where((kind == k)[:, None, None], by_tile, jnp.zeros_like(by_tile))
        cut = cut + jnp.einsum("ab,tib->tia", blocks[k], masked, preferred_element_type=jnp.float32)
    cut = cut.reshape(tiles, inst, nvar, tile).transpose(1, 2, 0, 3).reshape(state.shape)
    residual = local + cut + timewise
    return residual, state - time_step[None, None] * residual


def solution(mesh):
    placed = (
        P(("group", "inst"), None, "brick", None),
        P(("group", "brick"), None),
        P(),
        P("group"),
        P(("group", "brick"), None),
        P(("group", "brick"), None),
    )
    body = fused if mesh.shape["inst"] == 4 else plain
    return jax.shard_map(
        functools.partial(body, mesh),
        mesh=mesh,
        in_specs=placed,
        out_specs=(
            P(("group", "inst"), None, "brick", None),
            P(("group", "inst"), None, "brick", None),
        ),
        check_vma=False,
    )
```

```python
import functools
import math

import jax
import jax.numpy as jnp
from jax import lax
from jax.experimental import pallas as pl
from jax.experimental.pallas import tpu as pltpu
from jax.sharding import PartitionSpec as P

MESH = pl.DeviceIdType.MESH
GAMMA_MINUS = 0.4
EPS_FOURTH = 0.03125
CENTRE = (1.25, 0.0, 0.0, 0.0, 2.75)
LANES = 128


def spectral(m, count):
    m = m % count
    if m == 0 or 2 * m == count:
        return 0.0
    return (-1.0) ** m / math.tan(math.pi * m / count)


def flux_of(q):
    den, one, two, three, energy = q
    inv = 1.0 / den
    speed = one * inv
    press = GAMMA_MINUS * (energy - 0.5 * (one * one + two * two + three * three) * inv)
    return (one, one * speed + press, two * speed, three * speed, (energy + press) * speed)


def kernel(
    sizes, state, step_in, blocks_in, counts_in, index_in, kinds_in, acc, fresh,
    x, sib, send, cross, fwd, halo_out, halo_in, wide, xs, lhs, km, step, blocks, counts, index, kinds,
    in_sem, sib_send, sib_recv, cross_send, cross_recv, fwd_send, fwd_recv, halo_send, halo_recv, side_sem,
):
    inst, nvar, rows, cells, tile, total, chunks, n_brick = sizes
    width = cells // chunks
    ntypes = blocks.shape[0]
    group = lax.axis_index("group")
    me = lax.axis_index("inst")
    brick = lax.axis_index("brick")
    core = lax.rem(me, 2)
    chip = me // 2
    sibling = (group, chip * 2 + (1 - core), brick)
    partner = (group, (1 - chip) * 2 + core, brick)
    below = (group, me, brick - 1)
    above = (group, me, brick + 1)
    has_below = brick > 0
    has_above = brick < n_brick - 1

    def lanes(c):
        return pl.ds(pl.multiple_of(c * width, LANES), width)

    def fetch(c):
        return pltpu.make_async_copy(state.at[:, lanes(c)], x.at[:, lanes(c)], in_sem.at[c])

    def to_sibling(c):
        return pltpu.make_async_remote_copy(
            x.at[:, lanes(c)], sib.at[:, lanes(c)], sib_send.at[c], sib_recv.at[c], sibling, device_id_type=MESH)

    def to_partner(c):
        return pltpu.make_async_remote_copy(
            send.at[c], cross.at[c], cross_send.at[c], cross_recv.at[c], partner, device_id_type=MESH)

    def forward(c):
        return pltpu.make_async_remote_copy(
            cross.at[c], fwd.at[c], fwd_send.at[c], fwd_recv.at[c], sibling, device_id_type=MESH)

    def halo(side):
        return pltpu.make_async_remote_copy(
            halo_out.at[side], halo_in.at[side], halo_send.at[side], halo_recv.at[side],
            below if side == 0 else above, device_id_type=MESH)

    @pl.loop(0, chunks)
    def _(c):
        fetch(c).start()

    side = [
        pltpu.make_async_copy(a, b, side_sem.at[n])
        for n, (a, b) in enumerate((
            (counts_in, counts), (index_in, index), (kinds_in, kinds), (blocks_in, blocks), (step_in, step)))
    ]
    for copy in side:
        copy.start()

    barrier = pltpu.get_barrier_semaphore()
    pl.semaphore_signal(barrier, inc=1, device_id=sibling, device_id_type=MESH)
    pl.semaphore_signal(barrier, inc=1, device_id=partner, device_id_type=MESH)

    @pl.when(has_below)
    def _():
        pl.semaphore_signal(barrier, inc=1, device_id=below, device_id_type=MESH)

    @pl.when(has_above)
    def _():
        pl.semaphore_signal(barrier, inc=1, device_id=above, device_id_type=MESH)

    ends = n_brick - 1
    pl.semaphore_wait(barrier, 2 + (brick + ends) // n_brick + (ends - brick + ends) // n_brick)

    @pl.loop(0, chunks)
    def _(c):
        fetch(c).wait()
        for v in range(nvar):
            block = jnp.concatenate(
                [x[(i * nvar + v) * rows:(i * nvar + v + 1) * rows, lanes(c)] for i in range(inst)], axis=0)
            send[c, v * inst * rows:(v + 1) * inst * rows, :] = (block - CENTRE[v]).astype(jnp.bfloat16)
        to_partner(c).start()
        to_sibling(c).start()

    for v in range(nvar):
        for i in range(inst):
            at = (i * nvar + v) * rows
            halo_out[0, v, 2 * i:2 * i + 2, :] = x[at:at + 2, :]
            halo_out[1, v, 2 * i:2 * i + 2, :] = x[at + rows - 2:at + rows, :]

    @pl.when(has_below)
    def _():
        halo(0).start()

    @pl.when(has_above)
    def _():
        halo(1).start()

    for copy in side:
        copy.wait()
    per_row = cells // tile
    count = counts[brick]
    slots = index.shape[1]
    where_at = index[...]
    used = lax.broadcasted_iota(jnp.int32, (1, slots), 1) < count
    label = jnp.where(used, kinds[...] + 1, 0).astype(jnp.float32)
    tile_row = where_at // per_row
    tile_col = where_at - tile_row * per_row
    by_row = jnp.where(
        lax.broadcasted_iota(jnp.int32, (rows, slots), 0) == tile_row, label, 0.0).astype(jnp.bfloat16)
    by_col = jnp.where(
        lax.broadcasted_iota(jnp.int32, (per_row, slots), 0) == tile_col, 1.0, 0.0).astype(jnp.bfloat16)
    kind_map = lax.dot_general(
        by_row, by_col, (((1,), (1,)), ((), ())), preferred_element_type=jnp.float32).astype(jnp.bfloat16)
    spread = jnp.where(
        lax.broadcasted_iota(jnp.int32, (per_row, cells), 1) // tile
        == lax.broadcasted_iota(jnp.int32, (per_row, cells), 0), 1.0, 0.0).astype(jnp.bfloat16)
    kind_cells = jnp.dot(kind_map, spread, preferred_element_type=jnp.float32)

    groups = cells // LANES
    for g in range(groups):
        mask = kind_cells[:, g * LANES:(g + 1) * LANES]
        km[g * inst * rows:(g + 1) * inst * rows, :] = jnp.concatenate([mask] * inst, axis=0)
        for v in range(nvar):
            xs[g * inst * rows:(g + 1) * inst * rows, v * LANES:(v + 1) * LANES] = jnp.concatenate(
                [x[(i * nvar + v) * rows:(i * nvar + v + 1) * rows, g * LANES:(g + 1) * LANES]
                 for i in range(inst)], axis=0).astype(jnp.bfloat16)

    first = lax.broadcasted_iota(jnp.int32, (tile, LANES), 1) < tile

    @pl.loop(0, ntypes)
    def _(k):
        for out in range(nvar):
            for v in range(nvar):
                piece = blocks[k, out * tile:(out + 1) * tile, v * tile:(v + 1) * tile].astype(jnp.float32)
                both = jnp.concatenate([piece, piece], axis=1)
                at = out * LANES
                wide[k, at:at + tile, v * LANES:(v + 1) * LANES] = jnp.where(first, both, 0.0).astype(jnp.bfloat16)
                wide[k, at + tile:at + LANES, v * LANES:(v + 1) * LANES] = jnp.where(
                    first, 0.0, both).astype(jnp.bfloat16)

    parts = lhs.shape[0]
    depth = nvar * LANES

    @pl.loop(0, groups * inst * rows // parts)
    def _(m):
        at = pl.ds(pl.multiple_of(m * parts, parts), parts)
        kind_here = km[at, :]
        part = jnp.zeros((parts, depth), jnp.float32)
        for k in range(ntypes):
            keep = jnp.where(kind_here == k + 1.0, 1.0, 0.0).astype(jnp.bfloat16)
            for v in range(nvar):
                lhs[:, v * LANES:(v + 1) * LANES] = xs[at, v * LANES:(v + 1) * LANES] * keep
            part = part + lax.dot_general(
                lhs[...], wide[k], (((1,), (1,)), ((), ())), preferred_element_type=jnp.float32)
        per = parts // (inst * rows)
        for g in range(per):
            to = pl.ds(pl.multiple_of((m * per + g) * LANES, LANES), LANES)
            for i in range(inst):
                for v in range(nvar):
                    acc[(i * nvar + v) * rows:(i * nvar + v + 1) * rows, to] = part[
                        (g * inst + i) * rows:(g * inst + i + 1) * rows, v * LANES:(v + 1) * LANES]

    @pl.when(has_below)
    def _():
        halo(0).wait_send()
        halo(1).wait_recv()

    @pl.when(has_above)
    def _():
        halo(1).wait_send()
        halo(0).wait_recv()

    @pl.when(jnp.logical_not(has_below))
    def _():
        halo_in[1] = jnp.zeros(halo_in.shape[1:], jnp.float32)

    @pl.when(jnp.logical_not(has_above))
    def _():
        halo_in[0] = jnp.zeros(halo_in.shape[1:], jnp.float32)

    near = LANES

    @pl.loop(0, cells // near)
    def _(b):
        at = pl.ds(pl.multiple_of(b * near, LANES), near)
        for i in range(inst):
            full = []
            for v in range(nvar):
                full.append(jnp.concatenate([
                    halo_in[1, v, 2 * i:2 * i + 2, at],
                    x[(i * nvar + v) * rows:(i * nvar + v + 1) * rows, at],
                    halo_in[0, v, 2 * i:2 * i + 2, at],
                ], axis=0))
            safe = [jnp.where(full[0] == 0.0, 1.0, full[0])] + full[1:]
            flux = flux_of(safe)
            for v in range(nvar):
                q, f = full[v], flux[v]
                put = slice((i * nvar + v) * rows, (i * nvar + v + 1) * rows)
                acc[put, at] = acc[put, at] + 0.5 * (f[3:rows + 3] - f[1:rows + 1]) + EPS_FOURTH * (
                    q[4:] - 4.0 * q[3:-1] + 6.0 * q[2:-2] - 4.0 * q[1:-3] + q[:-4])

    def choose(a, b):
        return a if a == b else jnp.where(core == 0, a, b)

    span = range(1 - inst, inst)
    half = total // 2
    d_own = {m: spectral(m, total) for m in span}
    d_sib = {m: choose(spectral(m - inst, total), spectral(m + inst, total)) for m in span}
    d_cross = {m: spectral(m - half, total) for m in span}
    d_fwd = {m: choose(spectral(m - inst - half, total), spectral(m + inst - half, total)) for m in span}

    def finish(c):
        at = lanes(c)
        for v in range(nvar):
            cut = slice(v * inst * rows, (v + 1) * inst * rows)
            one = cross[c, cut, :].astype(jnp.float32)
            two = fwd[c, cut, :].astype(jnp.float32)
            for j in range(inst):
                put = slice((j * nvar + v) * rows, (j * nvar + v + 1) * rows)
                value = acc[put, at]
                for k in range(inst):
                    take = slice((k * nvar + v) * rows, (k * nvar + v + 1) * rows)
                    local = slice(k * rows, (k + 1) * rows)
                    m = j - k
                    if m:
                        value = value + d_own[m] * (x[take, at] - CENTRE[v])
                        value = value + d_cross[m] * one[local]
                    value = value + d_sib[m] * (sib[take, at] - CENTRE[v])
                    value = value + d_fwd[m] * two[local]
                acc[put, at] = value
                fresh[put, at] = x[put, at] - step[:, at] * value

    @pl.loop(0, chunks)
    def _(c):
        to_sibling(c).wait()
        to_partner(c).wait()
        forward(c).start()

        @pl.when(c > 0)
        def _():
            forward(c - 1).wait()
            finish(c - 1)

    forward(chunks - 1).wait()
    finish(chunks - 1)


def store(chunks, *refs):
    count = (len(refs) - 1) // 2
    sem = refs[-1]
    copies = []
    for n in range(count):
        rows = refs[n].shape[0] // chunks
        for c in range(chunks):
            at = pl.ds(c * rows, rows)
            copies.append(pltpu.make_async_copy(refs[n].at[at], refs[count + n].at[at], sem.at[n, c]))
    for copy in copies:
        copy.start()
    for copy in copies:
        copy.wait()


def fused(mesh, state, time_step, blocks, cut_counts, tile_index, tile_type):
    inst, nvar, rows, cells = state.shape
    tile = blocks.shape[1] // nvar
    total = inst * mesh.shape["inst"]
    n_brick = mesh.shape["brick"]
    chunks = 8
    all_rows = inst * nvar * rows
    width = cells // chunks
    depth = nvar * LANES
    product_rows = cells // LANES * inst * rows
    sizes = (inst, nvar, rows, cells, tile, total, chunks, n_brick)
    vmem = pl.BlockSpec(memory_space=pltpu.VMEM)
    hbm = pl.BlockSpec(memory_space=pltpu.HBM)
    anywhere = pl.BlockSpec(memory_space=pl.ANY)
    dma = pltpu.SemaphoreType.DMA
    flat = state.reshape(all_rows, cells)
    res, new = pl.pallas_call(
        functools.partial(kernel, sizes),
        out_shape=[pltpu.VMEM(flat.shape, jnp.float32)] * 2,
        in_specs=[hbm] * 6,
        out_specs=[vmem, vmem],
        scratch_shapes=[
            pltpu.VMEM((all_rows, cells), jnp.float32),
            pltpu.VMEM((all_rows, cells), jnp.float32),
            pltpu.VMEM((chunks, all_rows, width), jnp.bfloat16),
            pltpu.VMEM((chunks, all_rows, width), jnp.bfloat16),
            pltpu.VMEM((chunks, all_rows, width), jnp.bfloat16),
            pltpu.VMEM((2, nvar, 2 * inst, cells), jnp.float32),
            pltpu.VMEM((2, nvar, 2 * inst, cells), jnp.float32),
            pltpu.VMEM((blocks.shape[0], depth, depth), jnp.bfloat16),
            pltpu.VMEM((product_rows, depth), jnp.bfloat16),
            pltpu.VMEM((min(256, product_rows), depth), jnp.bfloat16),
            pltpu.VMEM((product_rows, LANES), jnp.float32),
            pltpu.VMEM(time_step.shape, jnp.float32),
            pltpu.VMEM(blocks.shape, blocks.dtype),
            pltpu.SMEM(cut_counts.shape, jnp.int32),
            pltpu.VMEM(tile_index.shape, jnp.int32),
            pltpu.VMEM(tile_type.shape, jnp.int32),
            dma((chunks,)), dma((chunks,)), dma((chunks,)), dma((chunks,)), dma((chunks,)),
            dma((chunks,)), dma((chunks,)), dma((2,)), dma((2,)), dma((5,)),
        ],
        compiler_params=pltpu.CompilerParams(
            collective_id=0, has_side_effects=True, vmem_limit_bytes=58 * 1024 * 1024 + 900 * 1024),
        cost_estimate=pl.CostEstimate(
            flops=2 * product_rows * depth * depth * blocks.shape[0], bytes_accessed=12 * all_rows * cells,
            transcendentals=0),
    )(flat, time_step, blocks, cut_counts, tile_index, tile_type)
    pieces = 4
    res, new = pl.pallas_call(
        functools.partial(store, pieces),
        out_shape=[jax.ShapeDtypeStruct(flat.shape, jnp.float32)] * 2,
        in_specs=[anywhere, anywhere],
        out_specs=[hbm, hbm],
        scratch_shapes=[dma((2, pieces))],
        compiler_params=pltpu.CompilerParams(vmem_limit_bytes=2 * 1024 * 1024),
    )(res, new)
    return res.reshape(state.shape), new.reshape(state.shape)


def plain(mesh, state, time_step, blocks, cut_counts, tile_index, tile_type):
    inst, nvar, rows, cells = state.shape
    tile = blocks.shape[1] // nvar
    size = mesh.shape["inst"]
    total = inst * size
    ends = mesh.shape["brick"] - 1
    tail = lax.ppermute(state[:, :, rows - 2:], "brick", [(i, i + 1) for i in range(ends)])
    head = lax.ppermute(state[:, :, :2], "brick", [(i + 1, i) for i in range(ends)])
    q = jnp.concatenate([tail, state, head], axis=2)
    density = jnp.where(q[:, 0] == 0.0, 1.0, q[:, 0])
    f = jnp.stack(flux_of((density, q[:, 1], q[:, 2], q[:, 3], q[:, 4])), axis=1)
    local = 0.5 * (f[:, :, 3:-1] - f[:, :, 1:-3]) + EPS_FOURTH * (
        q[:, :, 4:] - 4.0 * q[:, :, 3:-1] + 6.0 * q[:, :, 2:-2] - 4.0 * q[:, :, 1:-3] + q[:, :, :-4])
    table = jnp.asarray([spectral(m, total) for m in range(total)], jnp.float32)
    mine = lax.axis_index("inst") * inst + jnp.arange(inst)
    timewise = jnp.zeros(state.shape, jnp.float32)
    moving = state
    for hop in range(size):
        source = lax.rem(lax.axis_index("inst") + size - hop, size) * inst + jnp.arange(inst)
        coef = table[jnp.mod(mine[:, None] - source[None, :], total)]
        timewise = timewise + jnp.einsum("jk,kcxs->jcxs", coef, moving, precision=lax.Precision.HIGHEST)
        if hop < size - 1:
            moving = lax.ppermute(moving, "inst", [(i, (i + 1) % size) for i in range(size)])
    tiles = rows * cells // tile
    slots = jnp.arange(tile_index.shape[1])
    used = slots < cut_counts[lax.axis_index("brick")]
    label = jnp.where(used, tile_type[0], blocks.shape[0])
    hot = (tile_index[0][None, :] == jnp.arange(tiles)[:, None]) & used[None, :]
    kind = jnp.where(jnp.any(hot, axis=1), jnp.sum(jnp.where(hot, label[None, :], 0), axis=1), blocks.shape[0])
    by_tile = state.reshape(inst, nvar, tiles, tile).transpose(2, 0, 1, 3).reshape(tiles, inst, nvar * tile)
    by_tile = by_tile.astype(jnp.bfloat16)
    cut = jnp.zeros(by_tile.shape, jnp.float32)
    for k in range(blocks.shape[0]):
        masked = jnp.where((kind == k)[:, None, None], by_tile, jnp.zeros_like(by_tile))
        cut = cut + jnp.einsum("ab,tib->tia", blocks[k], masked, preferred_element_type=jnp.float32)
    cut = cut.reshape(tiles, inst, nvar, tile).transpose(1, 2, 0, 3).reshape(state.shape)
    residual = local + cut + timewise
    return residual, state - time_step[None, None] * residual


def solution(mesh):
    placed = (
        P(("group", "inst"), None, "brick", None),
        P(("group", "brick"), None),
        P(),
        P("group"),
        P(("group", "brick"), None),
        P(("group", "brick"), None),
    )
    body = fused if mesh.shape["inst"] == 4 else plain
    return jax.shard_map(
        functools.partial(body, mesh),
        mesh=mesh,
        in_specs=placed,
        out_specs=(
            P(("group", "inst"), None, "brick", None),
            P(("group", "inst"), None, "brick", None),
        ),
        check_vma=False,
    )
```

```python
import functools
import math

import jax
import jax.numpy as jnp
from jax import lax
from jax.experimental import pallas as pl
from jax.experimental.pallas import tpu as pltpu
from jax.sharding import PartitionSpec as P

MESH = pl.DeviceIdType.MESH
GAMMA_MINUS = 0.4
EPS_FOURTH = 0.03125
CENTRE = (1.25, 0.0, 0.0, 0.0, 2.75)
LANES = 128


def spectral(m, count):
    m = m % count
    if m == 0 or 2 * m == count:
        return 0.0
    return (-1.0) ** m / math.tan(math.pi * m / count)


def flux_of(q):
    den, one, two, three, energy = q
    inv = 1.0 / den
    speed = one * inv
    press = GAMMA_MINUS * (energy - 0.5 * (one * one + two * two + three * three) * inv)
    return (one, one * speed + press, two * speed, three * speed, (energy + press) * speed)


def kernel(
    sizes, state, step_in, blocks_in, counts_in, index_in, kinds_in, acc, fresh,
    x, sib, send, cross, fwd, halo_out, halo_in, wide, xs, lhs, km, step, blocks, counts, index, kinds,
    in_sem, sib_send, sib_recv, cross_send, cross_recv, fwd_send, fwd_recv, halo_send, halo_recv, side_sem,
):
    inst, nvar, rows, cells, tile, total, chunks, n_brick = sizes
    width = cells // chunks
    ntypes = blocks.shape[0]
    group = lax.axis_index("group")
    me = lax.axis_index("inst")
    brick = lax.axis_index("brick")
    core = lax.rem(me, 2)
    chip = me // 2
    sibling = (group, chip * 2 + (1 - core), brick)
    partner = (group, (1 - chip) * 2 + core, brick)
    below = (group, me, brick - 1)
    above = (group, me, brick + 1)
    has_below = brick > 0
    has_above = brick < n_brick - 1

    def lanes(c):
        return pl.ds(pl.multiple_of(c * width, LANES), width)

    def fetch(c):
        return pltpu.make_async_copy(state.at[:, lanes(c)], x.at[:, lanes(c)], in_sem.at[c])

    def to_sibling(c):
        return pltpu.make_async_remote_copy(
            x.at[:, lanes(c)], sib.at[:, lanes(c)], sib_send.at[c], sib_recv.at[c], sibling, device_id_type=MESH)

    def to_partner(c):
        return pltpu.make_async_remote_copy(
            send.at[c], cross.at[c], cross_send.at[c], cross_recv.at[c], partner, device_id_type=MESH)

    def forward(c):
        return pltpu.make_async_remote_copy(
            cross.at[c], fwd.at[c], fwd_send.at[c], fwd_recv.at[c], sibling, device_id_type=MESH)

    def halo(side):
        return pltpu.make_async_remote_copy(
            halo_out.at[side], halo_in.at[side], halo_send.at[side], halo_recv.at[side],
            below if side == 0 else above, device_id_type=MESH)

    fetch(0).start()

    barrier = pltpu.get_barrier_semaphore()
    pl.semaphore_signal(barrier, inc=1, device_id=sibling, device_id_type=MESH)
    pl.semaphore_signal(barrier, inc=1, device_id=partner, device_id_type=MESH)

    @pl.when(has_below)
    def _():
        pl.semaphore_signal(barrier, inc=1, device_id=below, device_id_type=MESH)

    @pl.when(has_above)
    def _():
        pl.semaphore_signal(barrier, inc=1, device_id=above, device_id_type=MESH)

    @pl.loop(1, chunks)
    def _(c):
        fetch(c).start()

    side = [
        pltpu.make_async_copy(a, b, side_sem.at[n])
        for n, (a, b) in enumerate((
            (counts_in, counts), (index_in, index), (kinds_in, kinds), (blocks_in, blocks), (step_in, step)))
    ]
    for copy in side:
        copy.start()

    def round_part(c):
        fetch(c).wait()
        for v in range(nvar):
            block = jnp.concatenate(
                [x[(i * nvar + v) * rows:(i * nvar + v + 1) * rows, lanes(c)] for i in range(inst)], axis=0)
            send[c, v * inst * rows:(v + 1) * inst * rows, :] = (block - CENTRE[v]).astype(jnp.bfloat16)

    round_part(0)
    ends = n_brick - 1
    pl.semaphore_wait(barrier, 2 + (brick + ends) // n_brick + (ends - brick + ends) // n_brick)
    to_partner(0).start()
    to_sibling(0).start()

    @pl.loop(1, chunks)
    def _(c):
        round_part(c)
        to_partner(c).start()
        to_sibling(c).start()

    for v in range(nvar):
        for i in range(inst):
            at = (i * nvar + v) * rows
            halo_out[0, v, 2 * i:2 * i + 2, :] = x[at:at + 2, :]
            halo_out[1, v, 2 * i:2 * i + 2, :] = x[at + rows - 2:at + rows, :]

    @pl.when(has_below)
    def _():
        halo(0).start()

    @pl.when(has_above)
    def _():
        halo(1).start()

    for copy in side:
        copy.wait()
    per_row = cells // tile
    count = counts[brick]
    slots = index.shape[1]
    where_at = index[...]
    used = lax.broadcasted_iota(jnp.int32, (1, slots), 1) < count
    label = jnp.where(used, kinds[...] + 1, 0).astype(jnp.float32)
    tile_row = where_at // per_row
    tile_col = where_at - tile_row * per_row
    by_row = jnp.where(
        lax.broadcasted_iota(jnp.int32, (rows, slots), 0) == tile_row, label, 0.0).astype(jnp.bfloat16)
    by_col = jnp.where(
        lax.broadcasted_iota(jnp.int32, (per_row, slots), 0) == tile_col, 1.0, 0.0).astype(jnp.bfloat16)
    kind_map = lax.dot_general(
        by_row, by_col, (((1,), (1,)), ((), ())), preferred_element_type=jnp.float32).astype(jnp.bfloat16)
    spread = jnp.where(
        lax.broadcasted_iota(jnp.int32, (per_row, cells), 1) // tile
        == lax.broadcasted_iota(jnp.int32, (per_row, cells), 0), 1.0, 0.0).astype(jnp.bfloat16)
    kind_cells = jnp.dot(kind_map, spread, preferred_element_type=jnp.float32)

    groups = cells // LANES
    for g in range(groups):
        mask = kind_cells[:, g * LANES:(g + 1) * LANES]
        km[g * inst * rows:(g + 1) * inst * rows, :] = jnp.concatenate([mask] * inst, axis=0)
        for v in range(nvar):
            xs[g * inst * rows:(g + 1) * inst * rows, v * LANES:(v + 1) * LANES] = jnp.concatenate(
                [x[(i * nvar + v) * rows:(i * nvar + v + 1) * rows, g * LANES:(g + 1) * LANES]
                 for i in range(inst)], axis=0).astype(jnp.bfloat16)

    first = lax.broadcasted_iota(jnp.int32, (tile, LANES), 1) < tile

    @pl.loop(0, ntypes)
    def _(k):
        for out in range(nvar):
            for v in range(nvar):
                piece = blocks[k, out * tile:(out + 1) * tile, v * tile:(v + 1) * tile].astype(jnp.float32)
                both = jnp.concatenate([piece, piece], axis=1)
                at = out * LANES
                wide[k, at:at + tile, v * LANES:(v + 1) * LANES] = jnp.where(first, both, 0.0).astype(jnp.bfloat16)
                wide[k, at + tile:at + LANES, v * LANES:(v + 1) * LANES] = jnp.where(
                    first, 0.0, both).astype(jnp.bfloat16)

    parts = lhs.shape[0]
    depth = nvar * LANES

    @pl.loop(0, groups * inst * rows // parts)
    def _(m):
        at = pl.ds(pl.multiple_of(m * parts, parts), parts)
        kind_here = km[at, :]
        part = jnp.zeros((parts, depth), jnp.float32)
        for k in range(ntypes):
            keep = jnp.where(kind_here == k + 1.0, 1.0, 0.0).astype(jnp.bfloat16)
            for v in range(nvar):
                lhs[:, v * LANES:(v + 1) * LANES] = xs[at, v * LANES:(v + 1) * LANES] * keep
            part = part + lax.dot_general(
                lhs[...], wide[k], (((1,), (1,)), ((), ())), preferred_element_type=jnp.float32)
        per = parts // (inst * rows)
        for g in range(per):
            to = pl.ds(pl.multiple_of((m * per + g) * LANES, LANES), LANES)
            for i in range(inst):
                for v in range(nvar):
                    acc[(i * nvar + v) * rows:(i * nvar + v + 1) * rows, to] = part[
                        (g * inst + i) * rows:(g * inst + i + 1) * rows, v * LANES:(v + 1) * LANES]

    @pl.when(has_below)
    def _():
        halo(0).wait_send()
        halo(1).wait_recv()

    @pl.when(has_above)
    def _():
        halo(1).wait_send()
        halo(0).wait_recv()

    @pl.when(jnp.logical_not(has_below))
    def _():
        halo_in[1] = jnp.zeros(halo_in.shape[1:], jnp.float32)

    @pl.when(jnp.logical_not(has_above))
    def _():
        halo_in[0] = jnp.zeros(halo_in.shape[1:], jnp.float32)

    near = LANES

    @pl.loop(0, cells // near)
    def _(b):
        at = pl.ds(pl.multiple_of(b * near, LANES), near)
        for i in range(inst):
            full = []
            for v in range(nvar):
                full.append(jnp.concatenate([
                    halo_in[1, v, 2 * i:2 * i + 2, at],
                    x[(i * nvar + v) * rows:(i * nvar + v + 1) * rows, at],
                    halo_in[0, v, 2 * i:2 * i + 2, at],
                ], axis=0))
            safe = [jnp.where(full[0] == 0.0, 1.0, full[0])] + full[1:]
            flux = flux_of(safe)
            for v in range(nvar):
                q, f = full[v], flux[v]
                put = slice((i * nvar + v) * rows, (i * nvar + v + 1) * rows)
                acc[put, at] = acc[put, at] + 0.5 * (f[3:rows + 3] - f[1:rows + 1]) + EPS_FOURTH * (
                    q[4:] - 4.0 * q[3:-1] + 6.0 * q[2:-2] - 4.0 * q[1:-3] + q[:-4])

    def choose(a, b):
        return a if a == b else jnp.where(core == 0, a, b)

    span = range(1 - inst, inst)
    half = total // 2
    d_own = {m: spectral(m, total) for m in span}
    d_sib = {m: choose(spectral(m - inst, total), spectral(m + inst, total)) for m in span}
    d_cross = {m: spectral(m - half, total) for m in span}
    d_fwd = {m: choose(spectral(m - inst - half, total), spectral(m + inst - half, total)) for m in span}

    def near_part(c):
        at = lanes(c)
        for v in range(nvar):
            for j in range(inst):
                put = slice((j * nvar + v) * rows, (j * nvar + v + 1) * rows)
                value = acc[put, at]
                for k in range(inst):
                    take = slice((k * nvar + v) * rows, (k * nvar + v + 1) * rows)
                    if j != k:
                        value = value + d_own[j - k] * (x[take, at] - CENTRE[v])
                    value = value + d_sib[j - k] * (sib[take, at] - CENTRE[v])
                acc[put, at] = value

    def far_part(c, source, table, last):
        at = lanes(c)
        for v in range(nvar):
            block = source[c, v * inst * rows:(v + 1) * inst * rows, :].astype(jnp.float32)
            for j in range(inst):
                put = slice((j * nvar + v) * rows, (j * nvar + v + 1) * rows)
                value = acc[put, at]
                for k in range(inst):
                    value = value + table[j - k] * block[k * rows:(k + 1) * rows]
                acc[put, at] = value
                if last:
                    fresh[put, at] = x[put, at] - step[:, at] * value

    @pl.loop(0, chunks)
    def _(c):
        to_sibling(c).wait()
        near_part(c)

    @pl.loop(0, chunks)
    def _(c):
        to_partner(c).wait()
        forward(c).start()
        far_part(c, cross, d_cross, False)

        @pl.when(c > 0)
        def _():
            forward(c - 1).wait()
            far_part(c - 1, fwd, d_fwd, True)

    forward(chunks - 1).wait()
    far_part(chunks - 1, fwd, d_fwd, True)


def store(chunks, *refs):
    count = (len(refs) - 1) // 2
    sem = refs[-1]
    copies = []
    for n in range(count):
        rows = refs[n].shape[0] // chunks
        for c in range(chunks):
            at = pl.ds(c * rows, rows)
            copies.append(pltpu.make_async_copy(refs[n].at[at], refs[count + n].at[at], sem.at[n, c]))
    for copy in copies:
        copy.start()
    for copy in copies:
        copy.wait()


def fused(mesh, state, time_step, blocks, cut_counts, tile_index, tile_type):
    inst, nvar, rows, cells = state.shape
    tile = blocks.shape[1] // nvar
    total = inst * mesh.shape["inst"]
    n_brick = mesh.shape["brick"]
    chunks = 8
    all_rows = inst * nvar * rows
    width = cells // chunks
    depth = nvar * LANES
    product_rows = cells // LANES * inst * rows
    sizes = (inst, nvar, rows, cells, tile, total, chunks, n_brick)
    vmem = pl.BlockSpec(memory_space=pltpu.VMEM)
    hbm = pl.BlockSpec(memory_space=pltpu.HBM)
    anywhere = pl.BlockSpec(memory_space=pl.ANY)
    dma = pltpu.SemaphoreType.DMA
    flat = state.reshape(all_rows, cells)
    res, new = pl.pallas_call(
        functools.partial(kernel, sizes),
        out_shape=[pltpu.VMEM(flat.shape, jnp.float32)] * 2,
        in_specs=[hbm] * 6,
        out_specs=[vmem, vmem],
        scratch_shapes=[
            pltpu.VMEM((all_rows, cells), jnp.float32),
            pltpu.VMEM((all_rows, cells), jnp.float32),
            pltpu.VMEM((chunks, all_rows, width), jnp.bfloat16),
            pltpu.VMEM((chunks, all_rows, width), jnp.bfloat16),
            pltpu.VMEM((chunks, all_rows, width), jnp.bfloat16),
            pltpu.VMEM((2, nvar, 2 * inst, cells), jnp.float32),
            pltpu.VMEM((2, nvar, 2 * inst, cells), jnp.float32),
            pltpu.VMEM((blocks.shape[0], depth, depth), jnp.bfloat16),
            pltpu.VMEM((product_rows, depth), jnp.bfloat16),
            pltpu.VMEM((min(256, product_rows), depth), jnp.bfloat16),
            pltpu.VMEM((product_rows, LANES), jnp.float32),
            pltpu.VMEM(time_step.shape, jnp.float32),
            pltpu.VMEM(blocks.shape, blocks.dtype),
            pltpu.SMEM(cut_counts.shape, jnp.int32),
            pltpu.VMEM(tile_index.shape, jnp.int32),
            pltpu.VMEM(tile_type.shape, jnp.int32),
            dma((chunks,)), dma((chunks,)), dma((chunks,)), dma((chunks,)), dma((chunks,)),
            dma((chunks,)), dma((chunks,)), dma((2,)), dma((2,)), dma((5,)),
        ],
        compiler_params=pltpu.CompilerParams(
            collective_id=0, has_side_effects=True, vmem_limit_bytes=58 * 1024 * 1024 + 900 * 1024),
        cost_estimate=pl.CostEstimate(
            flops=2 * product_rows * depth * depth * blocks.shape[0], bytes_accessed=12 * all_rows * cells,
            transcendentals=0),
    )(flat, time_step, blocks, cut_counts, tile_index, tile_type)
    pieces = 4
    res, new = pl.pallas_call(
        functools.partial(store, pieces),
        out_shape=[jax.ShapeDtypeStruct(flat.shape, jnp.float32)] * 2,
        in_specs=[anywhere, anywhere],
        out_specs=[hbm, hbm],
        scratch_shapes=[dma((2, pieces))],
        compiler_params=pltpu.CompilerParams(vmem_limit_bytes=2 * 1024 * 1024),
    )(res, new)
    return res.reshape(state.shape), new.reshape(state.shape)


def plain(mesh, state, time_step, blocks, cut_counts, tile_index, tile_type):
    inst, nvar, rows, cells = state.shape
    tile = blocks.shape[1] // nvar
    size = mesh.shape["inst"]
    total = inst * size
    ends = mesh.shape["brick"] - 1
    tail = lax.ppermute(state[:, :, rows - 2:], "brick", [(i, i + 1) for i in range(ends)])
    head = lax.ppermute(state[:, :, :2], "brick", [(i + 1, i) for i in range(ends)])
    q = jnp.concatenate([tail, state, head], axis=2)
    density = jnp.where(q[:, 0] == 0.0, 1.0, q[:, 0])
    f = jnp.stack(flux_of((density, q[:, 1], q[:, 2], q[:, 3], q[:, 4])), axis=1)
    local = 0.5 * (f[:, :, 3:-1] - f[:, :, 1:-3]) + EPS_FOURTH * (
        q[:, :, 4:] - 4.0 * q[:, :, 3:-1] + 6.0 * q[:, :, 2:-2] - 4.0 * q[:, :, 1:-3] + q[:, :, :-4])
    table = jnp.asarray([spectral(m, total) for m in range(total)], jnp.float32)
    mine = lax.axis_index("inst") * inst + jnp.arange(inst)
    timewise = jnp.zeros(state.shape, jnp.float32)
    moving = state
    for hop in range(size):
        source = lax.rem(lax.axis_index("inst") + size - hop, size) * inst + jnp.arange(inst)
        coef = table[jnp.mod(mine[:, None] - source[None, :], total)]
        timewise = timewise + jnp.einsum("jk,kcxs->jcxs", coef, moving, precision=lax.Precision.HIGHEST)
        if hop < size - 1:
            moving = lax.ppermute(moving, "inst", [(i, (i + 1) % size) for i in range(size)])
    tiles = rows * cells // tile
    slots = jnp.arange(tile_index.shape[1])
    used = slots < cut_counts[lax.axis_index("brick")]
    label = jnp.where(used, tile_type[0], blocks.shape[0])
    hot = (tile_index[0][None, :] == jnp.arange(tiles)[:, None]) & used[None, :]
    kind = jnp.where(jnp.any(hot, axis=1), jnp.sum(jnp.where(hot, label[None, :], 0), axis=1), blocks.shape[0])
    by_tile = state.reshape(inst, nvar, tiles, tile).transpose(2, 0, 1, 3).reshape(tiles, inst, nvar * tile)
    by_tile = by_tile.astype(jnp.bfloat16)
    cut = jnp.zeros(by_tile.shape, jnp.float32)
    for k in range(blocks.shape[0]):
        masked = jnp.where((kind == k)[:, None, None], by_tile, jnp.zeros_like(by_tile))
        cut = cut + jnp.einsum("ab,tib->tia", blocks[k], masked, preferred_element_type=jnp.float32)
    cut = cut.reshape(tiles, inst, nvar, tile).transpose(1, 2, 0, 3).reshape(state.shape)
    residual = local + cut + timewise
    return residual, state - time_step[None, None] * residual


def solution(mesh):
    placed = (
        P(("group", "inst"), None, "brick", None),
        P(("group", "brick"), None),
        P(),
        P("group"),
        P(("group", "brick"), None),
        P(("group", "brick"), None),
    )
    body = fused if mesh.shape["inst"] == 4 else plain
    return jax.shard_map(
        functools.partial(body, mesh),
        mesh=mesh,
        in_specs=placed,
        out_specs=(
            P(("group", "inst"), None, "brick", None),
            P(("group", "inst"), None, "brick", None),
        ),
        check_vma=False,
    )
```

```python
import functools
import math

import jax
import jax.numpy as jnp
from jax import lax
from jax.experimental import pallas as pl
from jax.experimental.pallas import tpu as pltpu
from jax.sharding import PartitionSpec as P

MESH = pl.DeviceIdType.MESH
GAMMA_MINUS = 0.4
EPS_FOURTH = 0.03125
CENTRE = (1.25, 0.0, 0.0, 0.0, 2.75)
LANES = 128


def spectral(m, count):
    m = m % count
    if m == 0 or 2 * m == count:
        return 0.0
    return (-1.0) ** m / math.tan(math.pi * m / count)


def flux_of(q):
    den, one, two, three, energy = q
    inv = 1.0 / den
    speed = one * inv
    press = GAMMA_MINUS * (energy - 0.5 * (one * one + two * two + three * three) * inv)
    return (one, one * speed + press, two * speed, three * speed, (energy + press) * speed)


def kernel(
    sizes, state, step_in, blocks_in, counts_in, index_in, kinds_in, acc, fresh,
    x, sib, send, cross, fwd, halo_out, halo_in, wide, xs, lhs, km, step, blocks, counts, index, kinds,
    in_sem, sib_send, sib_recv, cross_send, cross_recv, fwd_send, fwd_recv, halo_send, halo_recv, side_sem,
):
    inst, nvar, rows, cells, tile, total, chunks, n_brick = sizes
    width = cells // chunks
    ntypes = blocks.shape[0]
    group = lax.axis_index("group")
    me = lax.axis_index("inst")
    brick = lax.axis_index("brick")
    core = lax.rem(me, 2)
    chip = me // 2
    sibling = (group, chip * 2 + (1 - core), brick)
    partner = (group, (1 - chip) * 2 + core, brick)
    below = (group, me, brick - 1)
    above = (group, me, brick + 1)
    has_below = brick > 0
    has_above = brick < n_brick - 1

    def lanes(c):
        return pl.ds(pl.multiple_of(c * width, LANES), width)

    def fetch(c):
        return pltpu.make_async_copy(state.at[:, lanes(c)], x.at[:, lanes(c)], in_sem.at[c])

    def to_sibling(c):
        return pltpu.make_async_remote_copy(
            x.at[:, lanes(c)], sib.at[:, lanes(c)], sib_send.at[c], sib_recv.at[c], sibling, device_id_type=MESH)

    def to_partner(c):
        return pltpu.make_async_remote_copy(
            send.at[c], cross.at[c], cross_send.at[c], cross_recv.at[c], partner, device_id_type=MESH)

    def forward(c):
        return pltpu.make_async_remote_copy(
            cross.at[c], fwd.at[c], fwd_send.at[c], fwd_recv.at[c], sibling, device_id_type=MESH)

    def halo(side):
        return pltpu.make_async_remote_copy(
            halo_out.at[side], halo_in.at[side], halo_send.at[side], halo_recv.at[side],
            below if side == 0 else above, device_id_type=MESH)

    fetch(0).start()

    barrier = pltpu.get_barrier_semaphore()
    pl.semaphore_signal(barrier, inc=1, device_id=sibling, device_id_type=MESH)
    pl.semaphore_signal(barrier, inc=1, device_id=partner, device_id_type=MESH)

    @pl.when(has_below)
    def _():
        pl.semaphore_signal(barrier, inc=1, device_id=below, device_id_type=MESH)

    @pl.when(has_above)
    def _():
        pl.semaphore_signal(barrier, inc=1, device_id=above, device_id_type=MESH)

    @pl.loop(1, chunks)
    def _(c):
        fetch(c).start()

    side = [
        pltpu.make_async_copy(a, b, side_sem.at[n])
        for n, (a, b) in enumerate((
            (counts_in, counts), (index_in, index), (kinds_in, kinds), (blocks_in, blocks), (step_in, step)))
    ]
    for copy in side:
        copy.start()

    def round_part(c):
        fetch(c).wait()
        for v in range(nvar):
            block = jnp.concatenate(
                [x[(i * nvar + v) * rows:(i * nvar + v + 1) * rows, lanes(c)] for i in range(inst)], axis=0)
            send[c, v * inst * rows:(v + 1) * inst * rows, :] = (block - CENTRE[v]).astype(jnp.bfloat16)

    round_part(0)
    ends = n_brick - 1
    pl.semaphore_wait(barrier, 2 + (brick + ends) // n_brick + (ends - brick + ends) // n_brick)
    to_partner(0).start()
    to_sibling(0).start()

    @pl.loop(1, chunks)
    def _(c):
        round_part(c)
        to_partner(c).start()
        to_sibling(c).start()

    for v in range(nvar):
        for i in range(inst):
            at = (i * nvar + v) * rows
            halo_out[0, v, 2 * i:2 * i + 2, :] = x[at:at + 2, :]
            halo_out[1, v, 2 * i:2 * i + 2, :] = x[at + rows - 2:at + rows, :]

    @pl.when(has_below)
    def _():
        halo(0).start()

    @pl.when(has_above)
    def _():
        halo(1).start()

    for copy in side:
        copy.wait()
    per_row = cells // tile
    count = counts[brick]
    slots = index.shape[1]
    where_at = index[...]
    used = lax.broadcasted_iota(jnp.int32, (1, slots), 1) < count
    label = jnp.where(used, kinds[...] + 1, 0).astype(jnp.float32)
    tile_row = where_at // per_row
    tile_col = where_at - tile_row * per_row
    by_row = jnp.where(
        lax.broadcasted_iota(jnp.int32, (rows, slots), 0) == tile_row, label, 0.0).astype(jnp.bfloat16)
    by_col = jnp.where(
        lax.broadcasted_iota(jnp.int32, (per_row, slots), 0) == tile_col, 1.0, 0.0).astype(jnp.bfloat16)
    kind_map = lax.dot_general(
        by_row, by_col, (((1,), (1,)), ((), ())), preferred_element_type=jnp.float32).astype(jnp.bfloat16)
    spread = jnp.where(
        lax.broadcasted_iota(jnp.int32, (per_row, cells), 1) // tile
        == lax.broadcasted_iota(jnp.int32, (per_row, cells), 0), 1.0, 0.0).astype(jnp.bfloat16)
    kind_cells = jnp.dot(kind_map, spread, preferred_element_type=jnp.float32)

    groups = cells // LANES
    for g in range(groups):
        mask = kind_cells[:, g * LANES:(g + 1) * LANES]
        km[g * inst * rows:(g + 1) * inst * rows, :] = jnp.concatenate([mask] * inst, axis=0)
        for v in range(nvar):
            xs[g * inst * rows:(g + 1) * inst * rows, v * LANES:(v + 1) * LANES] = jnp.concatenate(
                [x[(i * nvar + v) * rows:(i * nvar + v + 1) * rows, g * LANES:(g + 1) * LANES]
                 for i in range(inst)], axis=0).astype(jnp.bfloat16)

    first = lax.broadcasted_iota(jnp.int32, (tile, LANES), 1) < tile

    @pl.loop(0, ntypes)
    def _(k):
        for out in range(nvar):
            for v in range(nvar):
                piece = blocks[k, out * tile:(out + 1) * tile, v * tile:(v + 1) * tile].astype(jnp.float32)
                both = jnp.concatenate([piece, piece], axis=1)
                at = out * LANES
                wide[k, at:at + tile, v * LANES:(v + 1) * LANES] = jnp.where(first, both, 0.0).astype(jnp.bfloat16)
                wide[k, at + tile:at + LANES, v * LANES:(v + 1) * LANES] = jnp.where(
                    first, 0.0, both).astype(jnp.bfloat16)

    parts = lhs.shape[0]
    depth = nvar * LANES

    @pl.loop(0, groups * inst * rows // parts)
    def _(m):
        at = pl.ds(pl.multiple_of(m * parts, parts), parts)
        kind_here = km[at, :]
        part = jnp.zeros((parts, depth), jnp.float32)
        for k in range(ntypes):
            keep = jnp.where(kind_here == k + 1.0, 1.0, 0.0).astype(jnp.bfloat16)
            for v in range(nvar):
                lhs[:, v * LANES:(v + 1) * LANES] = xs[at, v * LANES:(v + 1) * LANES] * keep
            part = part + lax.dot_general(
                lhs[...], wide[k], (((1,), (1,)), ((), ())), preferred_element_type=jnp.float32)
        per = parts // (inst * rows)
        for g in range(per):
            to = pl.ds(pl.multiple_of((m * per + g) * LANES, LANES), LANES)
            for i in range(inst):
                for v in range(nvar):
                    acc[(i * nvar + v) * rows:(i * nvar + v + 1) * rows, to] = part[
                        (g * inst + i) * rows:(g * inst + i + 1) * rows, v * LANES:(v + 1) * LANES]

    @pl.when(has_below)
    def _():
        halo(0).wait_send()
        halo(1).wait_recv()

    @pl.when(has_above)
    def _():
        halo(1).wait_send()
        halo(0).wait_recv()

    @pl.when(jnp.logical_not(has_below))
    def _():
        halo_in[1] = jnp.zeros(halo_in.shape[1:], jnp.float32)

    @pl.when(jnp.logical_not(has_above))
    def _():
        halo_in[0] = jnp.zeros(halo_in.shape[1:], jnp.float32)

    near = LANES

    @pl.loop(0, cells // near)
    def _(b):
        at = pl.ds(pl.multiple_of(b * near, LANES), near)
        for i in range(inst):
            full = []
            for v in range(nvar):
                full.append(jnp.concatenate([
                    halo_in[1, v, 2 * i:2 * i + 2, at],
                    x[(i * nvar + v) * rows:(i * nvar + v + 1) * rows, at],
                    halo_in[0, v, 2 * i:2 * i + 2, at],
                ], axis=0))
            safe = [jnp.where(full[0] == 0.0, 1.0, full[0])] + full[1:]
            flux = flux_of(safe)
            for v in range(nvar):
                q, f = full[v], flux[v]
                put = slice((i * nvar + v) * rows, (i * nvar + v + 1) * rows)
                acc[put, at] = acc[put, at] + 0.5 * (f[3:rows + 3] - f[1:rows + 1]) + EPS_FOURTH * (
                    q[4:] - 4.0 * q[3:-1] + 6.0 * q[2:-2] - 4.0 * q[1:-3] + q[:-4])

    def choose(a, b):
        return a if a == b else jnp.where(core == 0, a, b)

    span = range(1 - inst, inst)
    half = total // 2
    d_own = {m: spectral(m, total) for m in span}
    d_sib = {m: choose(spectral(m - inst, total), spectral(m + inst, total)) for m in span}
    d_cross = {m: spectral(m - half, total) for m in span}
    d_fwd = {m: choose(spectral(m - inst - half, total), spectral(m + inst - half, total)) for m in span}

    def near_part(c):
        at = lanes(c)
        for v in range(nvar):
            for j in range(inst):
                put = slice((j * nvar + v) * rows, (j * nvar + v + 1) * rows)
                value = acc[put, at]
                for k in range(inst):
                    take = slice((k * nvar + v) * rows, (k * nvar + v + 1) * rows)
                    if j != k:
                        value = value + d_own[j - k] * (x[take, at] - CENTRE[v])
                    value = value + d_sib[j - k] * (sib[take, at] - CENTRE[v])
                acc[put, at] = value

    def far_part(c, source, table, last):
        at = lanes(c)
        for v in range(nvar):
            block = source[c, v * inst * rows:(v + 1) * inst * rows, :].astype(jnp.float32)
            for j in range(inst):
                put = slice((j * nvar + v) * rows, (j * nvar + v + 1) * rows)
                value = acc[put, at]
                for k in range(inst):
                    value = value + table[j - k] * block[k * rows:(k + 1) * rows]
                acc[put, at] = value
                if last:
                    fresh[put, at] = x[put, at] - step[:, at] * value

    @pl.loop(0, chunks)
    def _(c):
        to_sibling(c).wait()
        near_part(c)

    @pl.loop(0, chunks)
    def _(c):
        to_partner(c).wait()
        forward(c).start()
        far_part(c, cross, d_cross, False)

        @pl.when(c > 0)
        def _():
            forward(c - 1).wait()
            far_part(c - 1, fwd, d_fwd, True)

    forward(chunks - 1).wait()
    far_part(chunks - 1, fwd, d_fwd, True)


def store(chunks, *refs):
    count = (len(refs) - 1) // 2
    sem = refs[-1]
    copies = []
    for n in range(count):
        rows = refs[n].shape[0] // chunks
        for c in range(chunks):
            at = pl.ds(c * rows, rows)
            copies.append(pltpu.make_async_copy(refs[n].at[at], refs[count + n].at[at], sem.at[n, c]))
    for copy in copies:
        copy.start()
    for copy in copies:
        copy.wait()


def fused(mesh, state, time_step, blocks, cut_counts, tile_index, tile_type):
    inst, nvar, rows, cells = state.shape
    tile = blocks.shape[1] // nvar
    total = inst * mesh.shape["inst"]
    n_brick = mesh.shape["brick"]
    chunks = 4
    all_rows = inst * nvar * rows
    width = cells // chunks
    depth = nvar * LANES
    product_rows = cells // LANES * inst * rows
    sizes = (inst, nvar, rows, cells, tile, total, chunks, n_brick)
    vmem = pl.BlockSpec(memory_space=pltpu.VMEM)
    hbm = pl.BlockSpec(memory_space=pltpu.HBM)
    anywhere = pl.BlockSpec(memory_space=pl.ANY)
    dma = pltpu.SemaphoreType.DMA
    flat = state.reshape(all_rows, cells)
    res, new = pl.pallas_call(
        functools.partial(kernel, sizes),
        out_shape=[pltpu.VMEM(flat.shape, jnp.float32)] * 2,
        in_specs=[hbm] * 6,
        out_specs=[vmem, vmem],
        scratch_shapes=[
            pltpu.VMEM((all_rows, cells), jnp.float32),
            pltpu.VMEM((all_rows, cells), jnp.float32),
            pltpu.VMEM((chunks, all_rows, width), jnp.bfloat16),
            pltpu.VMEM((chunks, all_rows, width), jnp.bfloat16),
            pltpu.VMEM((chunks, all_rows, width), jnp.bfloat16),
            pltpu.VMEM((2, nvar, 2 * inst, cells), jnp.float32),
            pltpu.VMEM((2, nvar, 2 * inst, cells), jnp.float32),
            pltpu.VMEM((blocks.shape[0], depth, depth), jnp.bfloat16),
            pltpu.VMEM((product_rows, depth), jnp.bfloat16),
            pltpu.VMEM((min(256, product_rows), depth), jnp.bfloat16),
            pltpu.VMEM((product_rows, LANES), jnp.float32),
            pltpu.VMEM(time_step.shape, jnp.float32),
            pltpu.VMEM(blocks.shape, blocks.dtype),
            pltpu.SMEM(cut_counts.shape, jnp.int32),
            pltpu.VMEM(tile_index.shape, jnp.int32),
            pltpu.VMEM(tile_type.shape, jnp.int32),
            dma((chunks,)), dma((chunks,)), dma((chunks,)), dma((chunks,)), dma((chunks,)),
            dma((chunks,)), dma((chunks,)), dma((2,)), dma((2,)), dma((5,)),
        ],
        compiler_params=pltpu.CompilerParams(
            collective_id=0, has_side_effects=True, vmem_limit_bytes=58 * 1024 * 1024 + 900 * 1024),
        cost_estimate=pl.CostEstimate(
            flops=2 * product_rows * depth * depth * blocks.shape[0], bytes_accessed=12 * all_rows * cells,
            transcendentals=0),
    )(flat, time_step, blocks, cut_counts, tile_index, tile_type)
    pieces = 4
    res, new = pl.pallas_call(
        functools.partial(store, pieces),
        out_shape=[jax.ShapeDtypeStruct(flat.shape, jnp.float32)] * 2,
        in_specs=[anywhere, anywhere],
        out_specs=[hbm, hbm],
        scratch_shapes=[dma((2, pieces))],
        compiler_params=pltpu.CompilerParams(vmem_limit_bytes=2 * 1024 * 1024),
    )(res, new)
    return res.reshape(state.shape), new.reshape(state.shape)


def plain(mesh, state, time_step, blocks, cut_counts, tile_index, tile_type):
    inst, nvar, rows, cells = state.shape
    tile = blocks.shape[1] // nvar
    size = mesh.shape["inst"]
    total = inst * size
    ends = mesh.shape["brick"] - 1
    tail = lax.ppermute(state[:, :, rows - 2:], "brick", [(i, i + 1) for i in range(ends)])
    head = lax.ppermute(state[:, :, :2], "brick", [(i + 1, i) for i in range(ends)])
    q = jnp.concatenate([tail, state, head], axis=2)
    density = jnp.where(q[:, 0] == 0.0, 1.0, q[:, 0])
    f = jnp.stack(flux_of((density, q[:, 1], q[:, 2], q[:, 3], q[:, 4])), axis=1)
    local = 0.5 * (f[:, :, 3:-1] - f[:, :, 1:-3]) + EPS_FOURTH * (
        q[:, :, 4:] - 4.0 * q[:, :, 3:-1] + 6.0 * q[:, :, 2:-2] - 4.0 * q[:, :, 1:-3] + q[:, :, :-4])
    table = jnp.asarray([spectral(m, total) for m in range(total)], jnp.float32)
    mine = lax.axis_index("inst") * inst + jnp.arange(inst)
    timewise = jnp.zeros(state.shape, jnp.float32)
    moving = state
    for hop in range(size):
        source = lax.rem(lax.axis_index("inst") + size - hop, size) * inst + jnp.arange(inst)
        coef = table[jnp.mod(mine[:, None] - source[None, :], total)]
        timewise = timewise + jnp.einsum("jk,kcxs->jcxs", coef, moving, precision=lax.Precision.HIGHEST)
        if hop < size - 1:
            moving = lax.ppermute(moving, "inst", [(i, (i + 1) % size) for i in range(size)])
    tiles = rows * cells // tile
    slots = jnp.arange(tile_index.shape[1])
    used = slots < cut_counts[lax.axis_index("brick")]
    label = jnp.where(used, tile_type[0], blocks.shape[0])
    hot = (tile_index[0][None, :] == jnp.arange(tiles)[:, None]) & used[None, :]
    kind = jnp.where(jnp.any(hot, axis=1), jnp.sum(jnp.where(hot, label[None, :], 0), axis=1), blocks.shape[0])
    by_tile = state.reshape(inst, nvar, tiles, tile).transpose(2, 0, 1, 3).reshape(tiles, inst, nvar * tile)
    by_tile = by_tile.astype(jnp.bfloat16)
    cut = jnp.zeros(by_tile.shape, jnp.float32)
    for k in range(blocks.shape[0]):
        masked = jnp.where((kind == k)[:, None, None], by_tile, jnp.zeros_like(by_tile))
        cut = cut + jnp.einsum("ab,tib->tia", blocks[k], masked, preferred_element_type=jnp.float32)
    cut = cut.reshape(tiles, inst, nvar, tile).transpose(1, 2, 0, 3).reshape(state.shape)
    residual = local + cut + timewise
    return residual, state - time_step[None, None] * residual


def solution(mesh):
    placed = (
        P(("group", "inst"), None, "brick", None),
        P(("group", "brick"), None),
        P(),
        P("group"),
        P(("group", "brick"), None),
        P(("group", "brick"), None),
    )
    body = fused if mesh.shape["inst"] == 4 else plain
    return jax.shard_map(
        functools.partial(body, mesh),
        mesh=mesh,
        in_specs=placed,
        out_specs=(
            P(("group", "inst"), None, "brick", None),
            P(("group", "inst"), None, "brick", None),
        ),
        check_vma=False,
    )
```
